32 devices in a mesh: groups: 2 (over x), row: 16 (over z, y, core).
Axes of the slice: x: 2, y: 2, z: 4, core: 2. Of those that a mesh axis runs over, the one named last changes fastest.
Arguments:
- tokens: bfloat16 [512, 4096], P('groups', 'row'), parts along dimension 0, may hold values from -6 to 6
- cotangent: bfloat16 [512, 4096], P('groups', 'row'), parts along dimension 0, may hold values from -6 to 6
- gate_weight: bfloat16 [4096, 14784], P(None, 'row'), may hold values from -0.125 to 0.125
- up_weight: bfloat16 [4096, 14784], P(None, 'row'), may hold values from -0.125 to 0.125
- down_weight: bfloat16 [14784, 4096], P('row'), may hold values from -0.0625 to 0.0625
Outputs:
- output: bfloat16 [512, 4096], P('groups', 'row'), parts along dimension 0
- input_grad: bfloat16 [512, 4096], P('groups', 'row'), parts along dimension 0
- gate_grad: bfloat16 [8192, 14784], P('groups', 'row'), parts along dimension 0
- up_grad: bfloat16 [8192, 14784], P('groups', 'row'), parts along dimension 0
- down_grad: bfloat16 [29568, 4096], P(('groups', 'row')), parts along dimension 0
The draws below stay inside these ranges and needn't reach their ends.
There are 2 independent parts, one for each index of `groups`. The reference program is written for one: setup_inputs(seed, part) draws one part's arguments, and reference() takes and returns one part's arrays. A program takes and returns all parts, laid end to end along the dimension named above; an argument that names none is the same for every part. Nothing has to cross between parts.
All inputs are finite; a program needn't handle non-finite values.
Results may differ from the reference program's by a relative error of at most 0.0051.
Values may be sent and summed in bfloat16 or wider, within the bound.
A program may use at most 128 MiB of HBM per device.

```python
import jax
import jax.numpy as jnp
from jax import lax

D = 4096
FF = 14784
TOKENS = 256


def spiked(array, own_key, source, target, shards_of, factor):
    def block_of(axis_at):
        return (jnp.arange(array.shape[axis_at]) // (array.shape[axis_at] // shards_of)).reshape((-1,) + (1,) * (array.ndim - 1 - axis_at))

    one_side = jax.random.permutation(own_key, shards_of)[block_of(target)]
    far = (block_of(target) + shards_of // 2) % shards_of
    return jnp.where((block_of(source) == one_side) | (block_of(source) == far), factor * array, array)


def shard_levels(own_key, dims, shards, smallest, top_value):
    level, own = 1.0, jax.random.fold_in(own_key, 6)
    for axis_at, blocks in shards:
        steps = jnp.exp(jax.random.uniform(jax.random.fold_in(own, axis_at), (blocks,), jnp.float32, smallest / len(shards), top_value / len(shards)))
        level = level * jnp.repeat(steps, dims[axis_at] // blocks).reshape([-1 if axis == axis_at else 1 for axis in range(len(dims))])
    return level


def noise(own_key, shape, deviation, most, pieces=(), dtype=jnp.bfloat16):
    drawn = deviation * jax.random.normal(own_key, shape, jnp.float32)
    if pieces:
        drawn = drawn * shard_levels(own_key, shape, pieces, -0.22, 0.18)
    return jnp.clip(drawn, -most, most).astype(dtype)


def heavy_noise(stream_key, shape, scale, reach, split, heavy, kind=jnp.bfloat16):
    values = scale * jax.random.normal(stream_key, shape, jnp.float32)
    if split:
        values = values * shard_levels(stream_key, shape, split, -0.22, 0.18)
    return jnp.clip(spiked(values, jax.random.fold_in(stream_key, 3), *heavy), -reach, reach).astype(kind)


def setup_inputs(seed: int = 0, part: int = 0) -> dict:
    key_of = jax.random.split(jax.random.key(seed), 6)
    part_splits = jax.random.split(jax.random.fold_in(key_of[5], part), 6)
    return {
        "tokens": noise(part_splits[0], (TOKENS, D), 1.0, 6.0, ((1, 16),)),
        "cotangent": noise(part_splits[1], (TOKENS, D), 1.0, 6.0, ((1, 16),)),
        "gate_weight": heavy_noise(key_of[2], (D, FF), D ** -0.5, 0.125, ((1, 16),), (1, 0, 16, 2.0)),
        "up_weight": heavy_noise(key_of[3], (D, FF), D ** -0.5, 0.125, ((1, 16),), (1, 0, 16, 2.0)),
        "down_weight": heavy_noise(key_of[4], (FF, D), FF ** -0.5, 0.0625, ((0, 16),), (0, 1, 16, 2.0)),
    }


def contract_rows(left, right):
    return lax.dot_general(left, right, (((0,), (0,)), ((), ())), preferred_element_type=jnp.float32)


def contract_cols(left, right):
    return lax.dot_general(left, right, (((1,), (1,)), ((), ())), preferred_element_type=jnp.float32)


def reference(tokens, cotangent, gate_weight, up_weight, down_weight):
    gate = jnp.dot(tokens, gate_weight, preferred_element_type=jnp.float32)
    up = jnp.dot(tokens, up_weight, preferred_element_type=jnp.float32)
    sig = jax.nn.sigmoid(gate)
    hidden = (gate * sig * up).astype(jnp.bfloat16)
    output = jnp.dot(hidden, down_weight, preferred_element_type=jnp.float32).astype(jnp.bfloat16)
    d_hidden = contract_cols(cotangent, down_weight)
    d_gate = (d_hidden * up * sig * (1.0 + gate * (1.0 - sig))).astype(jnp.bfloat16)
    d_up = (d_hidden * gate * sig).astype(jnp.bfloat16)
    input_grad = (contract_cols(d_gate, gate_weight) + contract_cols(d_up, up_weight)).astype(jnp.bfloat16)
    gate_grad = contract_rows(tokens, d_gate).astype(jnp.bfloat16)
    up_grad = contract_rows(tokens, d_up).astype(jnp.bfloat16)
    down_grad = contract_rows(hidden, cotangent).astype(jnp.bfloat16)
    return (output, input_grad, gate_grad, up_grad, down_grad)
```

```python
import functools

import jax
import jax.numpy as jnp
from jax import lax
from jax.experimental import pallas as pl
from jax.experimental.pallas import tpu as pltpu
from jax.sharding import PartitionSpec as P

F32, BF16 = jnp.float32, jnp.bfloat16
PLANES = 4


def contract_rows(left, right):
    return lax.dot_general(
        left, right, (((0,), (0,)), ((), ())), preferred_element_type=F32
    )


def contract_cols(left, right):
    return lax.dot_general(
        left, right, (((1,), (1,)), ((), ())), preferred_element_type=F32
    )


def kernel(
    x_in, dy_in, wg_hbm, wu_hbm, wd_hbm,
    out_ref, grad_ref, x_hbm, dy_hbm, h_hbm, dg_hbm, du_hbm,
    xg, dyg, wg, wu, wd, gate, up, dh, h, dg, du,
    keep, send_c, recv_c, send_y, recv_y, send_z, recv_z,
    wsem, az_s, az_r, ay_s, ay_r, ac_s, ac_r,
    rc_s, rc_r, ry_s, ry_r, rz_s, rz_r, osem,
):
    T, B = x_in.shape
    g = lax.axis_index("groups")
    me = lax.axis_index("row")
    c = lax.rem(me, 2)
    y = lax.rem(me // 2, 2)
    z = me // 4
    z0, z1 = lax.rem(z, 2), z // 2

    def plane(s):
        return lax.rem(z0 + s % 2, 2) + 2 * lax.rem(z1 + s // 2, 2)

    def index(zz, yy, cc):
        return (zz * 2 + yy) * 2 + cc

    def cols(block):
        return pl.ds(pl.multiple_of(block * B, B), B)

    def plane_ds(s):
        return pl.ds(pl.multiple_of(plane(s) * (4 * B), 4 * B), 4 * B)

    core_peer = (g, index(z, y, 1 - c))
    y_peer = (g, index(z, 1 - y, c))
    z_peer = [None] + [(g, index(plane(s), y, c)) for s in range(1, PLANES)]

    def weight_copy(w, s):
        sl = plane_ds(s)
        if w == 2:
            return pltpu.make_async_copy(wd_hbm.at[:, sl], wd.at[:, sl], wsem.at[2, s])
        src, dst = ((wg_hbm, wg), (wu_hbm, wu))[w]
        return pltpu.make_async_copy(src.at[sl], dst.at[sl], wsem.at[w, s])

    for s in range(PLANES):
        weight_copy(0, s).start()
        weight_copy(1, s).start()
    for s in range(PLANES):
        weight_copy(2, s).start()

    barrier = pltpu.get_barrier_semaphore()
    for peer in [core_peer, y_peer] + z_peer[1:]:
        pl.semaphore_signal(barrier, inc=1, device_id=peer, device_id_type=pl.DeviceIdType.MESH)
    pl.semaphore_wait(barrier, 5)

    def remote(src, dst, ss, rs, peer):
        return pltpu.make_async_remote_copy(
            src_ref=src, dst_ref=dst, send_sem=ss, recv_sem=rs,
            device_id=peer, device_id_type=pl.DeviceIdType.MESH,
        )

    ins, gathered = (x_in, dy_in), (xg, dyg)

    def gather_copy(a, kind, s, j=0):
        buf = gathered[a]
        lane = y if j == 0 else 1 - y
        sl = cols(index(plane(s), lane, c))
        src = ins[a] if (s == 0 and j == 0) else buf.at[:, sl]
        if kind == "z":
            return remote(ins[a], buf.at[:, cols(me)], az_s.at[a, s], az_r.at[a, s], z_peer[s])
        if kind == "y":
            return remote(src, buf.at[:, sl], ay_s.at[a, s], ay_r.at[a, s], y_peer)
        return remote(src, buf.at[:, sl], ac_s.at[a, 2 * s + j], ac_r.at[a, 2 * s + j], core_peer)

    def gather_begin(a):
        for s in range(1, PLANES):
            gather_copy(a, "z", s).start()
        gather_copy(a, "y", 0).start()
        gather_copy(a, "c", 0).start()
        gathered[a][:, cols(me)] = ins[a][...]

    def gather_z(a, s):
        buf, sl = gathered[a], cols(index(plane(s), y, c))
        remote(buf.at[:, sl], buf.at[:, sl], az_s.at[a, s], az_r.at[a, s], z_peer[s]).wait_recv()
        gather_copy(a, "y", s).start()
        gather_copy(a, "c", s, 0).start()

    def gather_y(a, s):
        buf, sl = gathered[a], cols(index(plane(s), 1 - y, c))
        remote(buf.at[:, sl], buf.at[:, sl], ay_s.at[a, s], ay_r.at[a, s], y_peer).wait_recv()
        gather_copy(a, "c", s, 1).start()

    def gather_ready(a, s):
        buf = gathered[a]
        for j, lane in ((0, y), (1, 1 - y)):
            sl = cols(index(plane(s), lane, 1 - c))
            remote(
                buf.at[:, sl], buf.at[:, sl], ac_s.at[a, 2 * s + j], ac_r.at[a, 2 * s + j], core_peer
            ).wait_recv()

    def forward(s):
        weight_copy(0, s).wait()
        weight_copy(1, s).wait()
        gather_ready(0, s)
        sl = plane_ds(s)
        x = xg[:, sl]
        gate_now = jnp.dot(x, wg[sl, :], preferred_element_type=F32)
        up_now = jnp.dot(x, wu[sl, :], preferred_element_type=F32)
        if s == 0:
            gate[...] = gate_now
            up[...] = up_now
        else:
            gate[...] += gate_now
            up[...] += up_now

    def backward(s):
        gather_ready(1, s)
        sl = plane_ds(s)
        now = contract_cols(dyg[:, sl], wd[:, sl])
        if s == 0:
            dh[...] = now
        else:
            dh[...] += now

    def reduce_c(a, s):
        return remote(send_c.at[a, s], recv_c.at[a, s], rc_s.at[a, s], rc_r.at[a, s], core_peer)

    def reduce_y(a, s):
        return remote(send_y.at[a, s], recv_y.at[a, s], ry_s.at[a, s], ry_r.at[a, s], y_peer)

    def reduce_z(a, s):
        return remote(send_z.at[a, s], recv_z.at[a, s], rz_s.at[a, s], rz_r.at[a, s], z_peer[s])

    def terms(a, block):
        sl = cols(block)
        if a == 0:
            return jnp.dot(h[...], wd[:, sl], preferred_element_type=F32)
        return contract_cols(dg[...], wg[sl, :]) + contract_cols(du[...], wu[sl, :])

    def stage_c(a, s):
        for j, lane in ((1, 1 - y), (0, y)):
            send_c[a, s, j] = terms(a, index(plane(s), lane, 1 - c)).astype(BF16)
        reduce_c(a, s).start()
        for j, lane in ((1, 1 - y), (0, y)):
            keep[a, s, j] = terms(a, index(plane(s), lane, c))

    def stage_y(a, s):
        reduce_c(a, s).wait_recv()
        send_y[a, s] = (keep[a, s, 1] + recv_c[a, s, 1].astype(F32)).astype(BF16)
        reduce_y(a, s).start()
        keep[a, s, 0] += recv_c[a, s, 0].astype(F32)

    def stage_z(a, s):
        reduce_y(a, s).wait_recv()
        now = keep[a, s, 0] + recv_y[a, s].astype(F32)
        if s == 0:
            keep[a, s, 0] = now
        else:
            send_z[a, s] = now.astype(BF16)
            reduce_z(a, s).start()

    def finish(a, ref):
        total = keep[a, 0, 0]
        for s in range(1, PLANES):
            reduce_z(a, s).wait_recv()
            total += recv_z[a, s].astype(F32)
        ref[...] = total.astype(BF16)

    far_first = (1, 2, 3, 0)
    gather_begin(0)
    gather_z(0, 1)
    gather_z(0, 2)
    gather_y(0, 0)
    gather_z(0, 3)
    gather_begin(1)
    gather_y(0, 1)
    forward(0)
    gather_y(0, 2)
    forward(1)
    gather_y(0, 3)
    forward(2)
    gather_z(1, 1)
    forward(3)
    gather_z(1, 2)
    gather_z(1, 3)
    gather_y(1, 0)

    chunk = 32

    @pl.loop(0, T // chunk)
    def _(i):
        rows = pl.ds(pl.multiple_of(i * chunk, chunk), chunk)
        gt, u = gate[rows, :], up[rows, :]
        h[rows, :] = (gt * jax.nn.sigmoid(gt) * u).astype(BF16)

    emits = [
        pltpu.make_async_copy(src, dst, osem.at[i])
        for i, (src, dst) in enumerate(
            ((xg, x_hbm), (dyg, dy_hbm), (h, h_hbm), (dg, dg_hbm), (du, du_hbm))
        )
    ]
    emits[0].start()
    emits[2].start()
    gather_y(1, 1)
    for s in range(PLANES):
        weight_copy(2, s).wait()
    stage_c(0, 1)
    gather_y(1, 2)
    stage_c(0, 2)
    gather_y(1, 3)
    stage_c(0, 3)
    stage_y(0, 1)
    stage_c(0, 0)
    stage_y(0, 2)
    backward(0)
    stage_y(0, 3)
    backward(1)
    stage_y(0, 0)
    backward(2)
    stage_z(0, 1)
    backward(3)
    stage_z(0, 2)

    @pl.loop(0, T // chunk)
    def _(i):
        rows = pl.ds(pl.multiple_of(i * chunk, chunk), chunk)
        gt, u, d = gate[rows, :], up[rows, :], dh[rows, :]
        sig = jax.nn.sigmoid(gt)
        dg[rows, :] = (d * u * sig * (1.0 + gt * (1.0 - sig))).astype(BF16)
        du[rows, :] = (d * gt * sig).astype(BF16)

    emits[1].start()
    emits[3].start()
    emits[4].start()
    stage_c(1, 1)
    stage_z(0, 3)
    stage_c(1, 2)
    stage_y(1, 1)
    stage_c(1, 3)
    stage_y(1, 2)
    stage_c(1, 0)
    stage_y(1, 3)
    stage_z(0, 0)
    stage_y(1, 0)
    finish(0, out_ref)
    for s in far_first:
        stage_z(1, s)
    finish(1, grad_ref)

    for emit in emits:
        emit.wait()
    for a in range(2):
        for s in range(PLANES):
            if s:
                gather_copy(a, "z", s).wait_send()
                reduce_z(a, s).wait_send()
            gather_copy(a, "y", s).wait_send()
            for j in range(2):
                gather_copy(a, "c", s, j).wait_send()
            reduce_c(a, s).wait_send()
            reduce_y(a, s).wait_send()


def fused(tokens, cotangent, gate_weight, up_weight, down_weight):
    T, B = tokens.shape
    D, F = gate_weight.shape
    vmem = pl.BlockSpec(memory_space=pltpu.VMEM)
    hbm = pl.BlockSpec(memory_space=pl.ANY)
    dma = pltpu.SemaphoreType.DMA

    def sds(*shape):
        return jax.ShapeDtypeStruct(shape, BF16)

    pair = (2, PLANES)
    return pl.pallas_call(
        kernel,
        out_shape=(sds(T, B), sds(T, B), sds(T, D), sds(T, D), sds(T, F), sds(T, F), sds(T, F)),
        in_specs=[vmem, vmem, hbm, hbm, hbm],
        out_specs=(vmem, vmem, hbm, hbm, hbm, hbm, hbm),
        scratch_shapes=[
            pltpu.VMEM((T, D), BF16),
            pltpu.VMEM((T, D), BF16),
            pltpu.VMEM((D, F), BF16),
            pltpu.VMEM((D, F), BF16),
            pltpu.VMEM((F, D), BF16),
            pltpu.VMEM((T, F), F32),
            pltpu.VMEM((T, F), F32),
            pltpu.VMEM((T, F), F32),
            pltpu.VMEM((T, F), BF16),
            pltpu.VMEM((T, F), BF16),
            pltpu.VMEM((T, F), BF16),
            pltpu.VMEM(pair + (2, T, B), F32),
            pltpu.VMEM(pair + (2, T, B), BF16),
            pltpu.VMEM(pair + (2, T, B), BF16),
            pltpu.VMEM(pair + (T, B), BF16),
            pltpu.VMEM(pair + (T, B), BF16),
            pltpu.VMEM(pair + (T, B), BF16),
            pltpu.VMEM(pair + (T, B), BF16),
            dma((3, PLANES)),
            dma(pair), dma(pair), dma(pair), dma(pair),
            dma((2, 2 * PLANES)), dma((2, 2 * PLANES)),
            dma(pair), dma(pair), dma(pair), dma(pair), dma(pair), dma(pair),
            dma((5,)),
        ],
        compiler_params=pltpu.CompilerParams(
            collective_id=0, has_side_effects=True, vmem_limit_bytes=60 * 2**20
        ),
        cost_estimate=pl.CostEstimate(
            flops=12 * T * D * F, bytes_accessed=6 * D * F + 10 * T * D, transcendentals=2 * T * F
        ),
        name="swiglu_fused",
    )(tokens, cotangent, gate_weight, up_weight, down_weight)


def on_device_fused(tokens, cotangent, gate_weight, up_weight, down_weight):
    output, input_grad, whole_x, whole_dy, hidden, d_gate, d_up = fused(
        tokens, cotangent, gate_weight, up_weight, down_weight
    )
    gate_grad = contract_rows(whole_x, d_gate).astype(BF16)
    up_grad = contract_rows(whole_x, d_up).astype(BF16)
    down_grad = contract_rows(hidden, whole_dy).astype(BF16)
    return (output, input_grad, gate_grad, up_grad, down_grad)


def on_device(tokens, cotangent, gate_weight, up_weight, down_weight):
    whole_x = lax.all_gather(tokens, "row", axis=1, tiled=True)
    gate = jnp.dot(whole_x, gate_weight, preferred_element_type=F32)
    up = jnp.dot(whole_x, up_weight, preferred_element_type=F32)
    sig = jax.nn.sigmoid(gate)
    hidden = (gate * sig * up).astype(BF16)
    out_terms = jnp.dot(hidden, down_weight, preferred_element_type=F32)
    output = lax.psum_scatter(out_terms, "row", scatter_dimension=1, tiled=True).astype(BF16)
    whole_dy = lax.all_gather(cotangent, "row", axis=1, tiled=True)
    d_hidden = contract_cols(whole_dy, down_weight)
    d_gate = (d_hidden * up * sig * (1.0 + gate * (1.0 - sig))).astype(BF16)
    d_up = (d_hidden * gate * sig).astype(BF16)
    gate_grad = contract_rows(whole_x, d_gate).astype(BF16)
    up_grad = contract_rows(whole_x, d_up).astype(BF16)
    down_grad = contract_rows(hidden, whole_dy).astype(BF16)
    grad_terms = contract_cols(d_gate, gate_weight) + contract_cols(d_up, up_weight)
    input_grad = lax.psum_scatter(grad_terms, "row", scatter_dimension=1, tiled=True).astype(BF16)
    return (output, input_grad, gate_grad, up_grad, down_grad)


def local(rows, tokens, cotangent, gate_weight, up_weight, down_weight):
    fits = rows == 4 * PLANES and tokens.shape[1] % 128 == 0 and tokens.shape[0] % 32 == 0
    body = on_device_fused if fits else on_device
    return body(tokens, cotangent, gate_weight, up_weight, down_weight)


def solution(mesh):
    placed = (
        P("groups", "row"),
        P("groups", "row"),
        P(None, "row"),
        P(None, "row"),
        P("row", None),
    )
    return jax.shard_map(
        functools.partial(local, mesh.shape["row"]),
        mesh=mesh,
        in_specs=placed,
        out_specs=(
            P("groups", "row"),
            P("groups", "row"),
            P("groups", "row"),
            P("groups", "row"),
            P(("groups", "row"), None),
        ),
        check_vma=False,
    )
```

```python
import functools

import jax
import jax.numpy as jnp
from jax import lax
from jax.experimental import pallas as pl
from jax.experimental.pallas import tpu as pltpu
from jax.sharding import PartitionSpec as P

F32, BF16 = jnp.float32, jnp.bfloat16
PLANES = 4


def contract_rows(left, right):
    return lax.dot_general(
        left, right, (((0,), (0,)), ((), ())), preferred_element_type=F32
    )


def contract_cols(left, right):
    return lax.dot_general(
        left, right, (((1,), (1,)), ((), ())), preferred_element_type=F32
    )


def kernel(
    x_in, dy_in, wg_hbm, wu_hbm, wd_hbm,
    out_ref, grad_ref, x_hbm, dy_hbm, h_hbm, dg_hbm, du_hbm,
    xg, dyg, wg, wu, wd, gate, up, dh, h, dg, du,
    keep, send_c, recv_c, send_y, recv_y, send_z, recv_z,
    wsem, az_s, az_r, ay_s, ay_r, ac_s, ac_r,
    rc_s, rc_r, ry_s, ry_r, rz_s, rz_r, osem,
):
    T, B = x_in.shape
    g = lax.axis_index("groups")
    me = lax.axis_index("row")
    c = lax.rem(me, 2)
    y = lax.rem(me // 2, 2)
    z = me // 4
    z0, z1 = lax.rem(z, 2), z // 2

    def plane(s):
        return lax.rem(z0 + s % 2, 2) + 2 * lax.rem(z1 + s // 2, 2)

    def index(zz, yy, cc):
        return (zz * 2 + yy) * 2 + cc

    def cols(block):
        return pl.ds(pl.multiple_of(block * B, B), B)

    def plane_ds(s):
        return pl.ds(pl.multiple_of(plane(s) * (4 * B), 4 * B), 4 * B)

    core_peer = (g, index(z, y, 1 - c))
    y_peer = (g, index(z, 1 - y, c))
    z_peer = [None] + [(g, index(plane(s), y, c)) for s in range(1, PLANES)]

    def weight_copy(w, s):
        sl = plane_ds(s)
        src, dst = ((wg_hbm, wg), (wu_hbm, wu), (wd_hbm, wd))[w]
        return pltpu.make_async_copy(src.at[:, sl], dst.at[:, sl], wsem.at[w, s])

    for s in range(PLANES):
        weight_copy(0, s).start()
        weight_copy(1, s).start()
    for s in range(PLANES):
        weight_copy(2, s).start()

    barrier = pltpu.get_barrier_semaphore()
    for peer in [core_peer, y_peer] + z_peer[1:]:
        pl.semaphore_signal(barrier, inc=1, device_id=peer, device_id_type=pl.DeviceIdType.MESH)
    pl.semaphore_wait(barrier, 5)

    def remote(src, dst, ss, rs, peer):
        return pltpu.make_async_remote_copy(
            src_ref=src, dst_ref=dst, send_sem=ss, recv_sem=rs,
            device_id=peer, device_id_type=pl.DeviceIdType.MESH,
        )

    ins, gathered = (x_in, dy_in), (xg, dyg)

    def gather_copy(a, kind, s, j=0):
        buf = gathered[a]
        lane = y if j == 0 else 1 - y
        sl = cols(index(plane(s), lane, c))
        src = ins[a] if (s == 0 and j == 0) else buf.at[:, sl]
        if kind == "z":
            return remote(ins[a], buf.at[:, cols(me)], az_s.at[a, s], az_r.at[a, s], z_peer[s])
        if kind == "y":
            return remote(src, buf.at[:, sl], ay_s.at[a, s], ay_r.at[a, s], y_peer)
        return remote(src, buf.at[:, sl], ac_s.at[a, 2 * s + j], ac_r.at[a, 2 * s + j], core_peer)

    def gather_begin(a):
        for s in range(1, PLANES):
            gather_copy(a, "z", s).start()
        gather_copy(a, "y", 0).start()
        gather_copy(a, "c", 0).start()
        gathered[a][:, cols(me)] = ins[a][...]

    def gather_z(a, s):
        buf, sl = gathered[a], cols(index(plane(s), y, c))
        remote(buf.at[:, sl], buf.at[:, sl], az_s.at[a, s], az_r.at[a, s], z_peer[s]).wait_recv()
        gather_copy(a, "y", s).start()
        gather_copy(a, "c", s, 0).start()

    def gather_y(a, s):
        buf, sl = gathered[a], cols(index(plane(s), 1 - y, c))
        remote(buf.at[:, sl], buf.at[:, sl], ay_s.at[a, s], ay_r.at[a, s], y_peer).wait_recv()
        gather_copy(a, "c", s, 1).start()

    def gather_ready(a, s):
        buf = gathered[a]
        for j, lane in ((0, y), (1, 1 - y)):
            sl = cols(index(plane(s), lane, 1 - c))
            remote(
                buf.at[:, sl], buf.at[:, sl], ac_s.at[a, 2 * s + j], ac_r.at[a, 2 * s + j], core_peer
            ).wait_recv()

    def forward(s):
        weight_copy(0, s).wait()
        weight_copy(1, s).wait()
        gather_ready(0, s)
        sl = plane_ds(s)
        x = xg[:, sl]
        gate_now = contract_cols(x, wg[:, sl])
        up_now = contract_cols(x, wu[:, sl])
        if s == 0:
            gate[...] = gate_now
            up[...] = up_now
        else:
            gate[...] += gate_now
            up[...] += up_now

    def backward(s):
        gather_ready(1, s)
        sl = plane_ds(s)
        now = contract_cols(dyg[:, sl], wd[:, sl])
        if s == 0:
            dh[...] = now
        else:
            dh[...] += now

    def reduce_c(a, s):
        return remote(send_c.at[a, s], recv_c.at[a, s], rc_s.at[a, s], rc_r.at[a, s], core_peer)

    def reduce_y(a, s):
        return remote(send_y.at[a, s], recv_y.at[a, s], ry_s.at[a, s], ry_r.at[a, s], y_peer)

    def reduce_z(a, s):
        return remote(send_z.at[a, s], recv_z.at[a, s], rz_s.at[a, s], rz_r.at[a, s], z_peer[s])

    def terms(a, block):
        sl = cols(block)
        if a == 0:
            return jnp.dot(h[...], wd[:, sl], preferred_element_type=F32)
        return jnp.dot(dg[...], wg[:, sl], preferred_element_type=F32) + jnp.dot(
            du[...], wu[:, sl], preferred_element_type=F32
        )

    def stage_c(a, s):
        for j, lane in ((1, 1 - y), (0, y)):
            send_c[a, s, j] = terms(a, index(plane(s), lane, 1 - c)).astype(BF16)
        reduce_c(a, s).start()
        for j, lane in ((1, 1 - y), (0, y)):
            keep[a, s, j] = terms(a, index(plane(s), lane, c))

    def stage_y(a, s):
        reduce_c(a, s).wait_recv()
        send_y[a, s] = (keep[a, s, 1] + recv_c[a, s, 1].astype(F32)).astype(BF16)
        reduce_y(a, s).start()
        keep[a, s, 0] += recv_c[a, s, 0].astype(F32)

    def stage_z(a, s):
        reduce_y(a, s).wait_recv()
        now = keep[a, s, 0] + recv_y[a, s].astype(F32)
        if s == 0:
            keep[a, s, 0] = now
        else:
            send_z[a, s] = now.astype(BF16)
            reduce_z(a, s).start()

    def finish(a, ref):
        total = keep[a, 0, 0]
        for s in range(1, PLANES):
            reduce_z(a, s).wait_recv()
            total += recv_z[a, s].astype(F32)
        ref[...] = total.astype(BF16)

    far_first = (1, 2, 3, 0)
    gather_begin(0)
    gather_z(0, 1)
    gather_z(0, 2)
    gather_y(0, 0)
    gather_z(0, 3)
    gather_begin(1)
    gather_y(0, 1)
    forward(0)
    gather_y(0, 2)
    forward(1)
    gather_y(0, 3)
    forward(2)
    gather_z(1, 1)
    forward(3)
    gather_z(1, 2)
    gather_z(1, 3)
    gather_y(1, 0)

    chunk = 32

    @pl.loop(0, T // chunk)
    def _(i):
        rows = pl.ds(pl.multiple_of(i * chunk, chunk), chunk)
        gt, u = gate[rows, :], up[rows, :]
        h[rows, :] = (gt * jax.nn.sigmoid(gt) * u).astype(BF16)

    emits = [
        pltpu.make_async_copy(src, dst, osem.at[i])
        for i, (src, dst) in enumerate(
            ((xg, x_hbm), (dyg, dy_hbm), (h, h_hbm), (dg, dg_hbm), (du, du_hbm))
        )
    ]
    emits[0].start()
    emits[2].start()
    gather_y(1, 1)
    for s in range(PLANES):
        weight_copy(2, s).wait()
    stage_c(0, 1)
    gather_y(1, 2)
    stage_c(0, 2)
    gather_y(1, 3)
    stage_c(0, 3)
    stage_y(0, 1)
    stage_c(0, 0)
    stage_y(0, 2)
    backward(0)
    stage_y(0, 3)
    backward(1)
    stage_y(0, 0)
    backward(2)
    stage_z(0, 1)
    backward(3)
    stage_z(0, 2)

    @pl.loop(0, T // chunk)
    def _(i):
        rows = pl.ds(pl.multiple_of(i * chunk, chunk), chunk)
        gt, u, d = gate[rows, :], up[rows, :], dh[rows, :]
        sig = jax.nn.sigmoid(gt)
        dg[rows, :] = (d * u * sig * (1.0 + gt * (1.0 - sig))).astype(BF16)
        du[rows, :] = (d * gt * sig).astype(BF16)

    emits[1].start()
    emits[3].start()
    emits[4].start()
    stage_c(1, 1)
    stage_z(0, 3)
    stage_c(1, 2)
    stage_y(1, 1)
    stage_c(1, 3)
    stage_y(1, 2)
    stage_c(1, 0)
    stage_y(1, 3)
    stage_z(0, 0)
    stage_y(1, 0)
    finish(0, out_ref)
    for s in far_first:
        stage_z(1, s)
    finish(1, grad_ref)

    for emit in emits:
        emit.wait()
    for a in range(2):
        for s in range(PLANES):
            if s:
                gather_copy(a, "z", s).wait_send()
                reduce_z(a, s).wait_send()
            gather_copy(a, "y", s).wait_send()
            for j in range(2):
                gather_copy(a, "c", s, j).wait_send()
            reduce_c(a, s).wait_send()
            reduce_y(a, s).wait_send()


def fused(tokens, cotangent, gate_weight, up_weight, down_weight):
    T, B = tokens.shape
    F, D = down_weight.shape
    vmem = pl.BlockSpec(memory_space=pltpu.VMEM)
    hbm = pl.BlockSpec(memory_space=pl.ANY)
    dma = pltpu.SemaphoreType.DMA

    def sds(*shape):
        return jax.ShapeDtypeStruct(shape, BF16)

    pair = (2, PLANES)
    return pl.pallas_call(
        kernel,
        out_shape=(sds(T, B), sds(T, B), sds(T, D), sds(T, D), sds(T, F), sds(T, F), sds(T, F)),
        in_specs=[vmem, vmem, hbm, hbm, hbm],
        out_specs=(vmem, vmem, hbm, hbm, hbm, hbm, hbm),
        scratch_shapes=[
            pltpu.VMEM((T, D), BF16),
            pltpu.VMEM((T, D), BF16),
            pltpu.VMEM((F, D), BF16),
            pltpu.VMEM((F, D), BF16),
            pltpu.VMEM((F, D), BF16),
            pltpu.VMEM((T, F), F32),
            pltpu.VMEM((T, F), F32),
            pltpu.VMEM((T, F), F32),
            pltpu.VMEM((T, F), BF16),
            pltpu.VMEM((T, F), BF16),
            pltpu.VMEM((T, F), BF16),
            pltpu.VMEM(pair + (2, T, B), F32),
            pltpu.VMEM(pair + (2, T, B), BF16),
            pltpu.VMEM(pair + (2, T, B), BF16),
            pltpu.VMEM(pair + (T, B), BF16),
            pltpu.VMEM(pair + (T, B), BF16),
            pltpu.VMEM(pair + (T, B), BF16),
            pltpu.VMEM(pair + (T, B), BF16),
            dma((3, PLANES)),
            dma(pair), dma(pair), dma(pair), dma(pair),
            dma((2, 2 * PLANES)), dma((2, 2 * PLANES)),
            dma(pair), dma(pair), dma(pair), dma(pair), dma(pair), dma(pair),
            dma((5,)),
        ],
        compiler_params=pltpu.CompilerParams(
            collective_id=0, has_side_effects=True, vmem_limit_bytes=60 * 2**20
        ),
        cost_estimate=pl.CostEstimate(
            flops=12 * T * D * F, bytes_accessed=6 * D * F + 10 * T * D, transcendentals=2 * T * F
        ),
        name="swiglu_fused",
    )(tokens, cotangent, gate_weight.T, up_weight.T, down_weight)


def gradient_kernel(x, dy, h, dg, du, gate_out, up_out, down_out, left, right):
    phase, step = pl.program_id(0), pl.program_id(1)

    @pl.when((phase == 0) & (step == 0))
    def _():
        left[...] = dg[...].T
        right[...] = du[...].T

    @pl.when((phase == 1) & (step == 0))
    def _():
        left[...] = h[...].T

    @pl.when(phase == 0)
    def _():
        gate_out[...] = jnp.dot(left[...], x[...], preferred_element_type=F32).astype(BF16)
        up_out[...] = jnp.dot(right[...], x[...], preferred_element_type=F32).astype(BF16)

    @pl.when(phase == 1)
    def _():
        down_out[...] = jnp.dot(left[...], dy[...], preferred_element_type=F32).astype(BF16)


def gradients(x, dy, h, dg, du):
    T, D = x.shape
    F = h.shape[1]
    width = 512
    steps = D // width

    def first(p, j):
        return (0, jnp.where(p == 0, j, steps - 1))

    def second(p, j):
        return (0, jnp.where(p == 0, 0, j))

    def whole(p, j):
        return (0, 0)

    out = jax.ShapeDtypeStruct((F, D), BF16)
    return pl.pallas_call(
        gradient_kernel,
        grid=(2, steps),
        out_shape=(out, out, out),
        in_specs=[
            pl.BlockSpec((T, width), first),
            pl.BlockSpec((T, width), second),
            pl.BlockSpec((T, F), whole),
            pl.BlockSpec((T, F), whole),
            pl.BlockSpec((T, F), whole),
        ],
        out_specs=(
            pl.BlockSpec((F, width), first),
            pl.BlockSpec((F, width), first),
            pl.BlockSpec((F, width), second),
        ),
        scratch_shapes=[pltpu.VMEM((F, T), BF16), pltpu.VMEM((F, T), BF16)],
        compiler_params=pltpu.CompilerParams(vmem_limit_bytes=60 * 2**20),
        cost_estimate=pl.CostEstimate(
            flops=6 * T * D * F, bytes_accessed=6 * D * F + 4 * T * D, transcendentals=0
        ),
        name="weight_gradients",
    )(x, dy, h, dg, du)


def on_device_fused(tokens, cotangent, gate_weight, up_weight, down_weight):
    output, input_grad, whole_x, whole_dy, hidden, d_gate, d_up = fused(
        tokens, cotangent, gate_weight, up_weight, down_weight
    )
    gate_grad, up_grad, down_grad = gradients(whole_x, whole_dy, hidden, d_gate, d_up)
    return (output, input_grad, gate_grad.T, up_grad.T, down_grad)


def on_device(tokens, cotangent, gate_weight, up_weight, down_weight):
    whole_x = lax.all_gather(tokens, "row", axis=1, tiled=True)
    gate = jnp.dot(whole_x, gate_weight, preferred_element_type=F32)
    up = jnp.dot(whole_x, up_weight, preferred_element_type=F32)
    sig = jax.nn.sigmoid(gate)
    hidden = (gate * sig * up).astype(BF16)
    out_terms = jnp.dot(hidden, down_weight, preferred_element_type=F32)
    output = lax.psum_scatter(out_terms, "row", scatter_dimension=1, tiled=True).astype(BF16)
    whole_dy = lax.all_gather(cotangent, "row", axis=1, tiled=True)
    d_hidden = contract_cols(whole_dy, down_weight)
    d_gate = (d_hidden * up * sig * (1.0 + gate * (1.0 - sig))).astype(BF16)
    d_up = (d_hidden * gate * sig).astype(BF16)
    gate_grad = contract_rows(whole_x, d_gate).astype(BF16)
    up_grad = contract_rows(whole_x, d_up).astype(BF16)
    down_grad = contract_rows(hidden, whole_dy).astype(BF16)
    grad_terms = contract_cols(d_gate, gate_weight) + contract_cols(d_up, up_weight)
    input_grad = lax.psum_scatter(grad_terms, "row", scatter_dimension=1, tiled=True).astype(BF16)
    return (output, input_grad, gate_grad, up_grad, down_grad)


def local(rows, tokens, cotangent, gate_weight, up_weight, down_weight):
    fits = rows == 4 * PLANES and tokens.shape[1] % 128 == 0 and tokens.shape[0] % 32 == 0
    body = on_device_fused if fits else on_device
    return body(tokens, cotangent, gate_weight, up_weight, down_weight)


def solution(mesh):
    placed = (
        P("groups", "row"),
        P("groups", "row"),
        P(None, "row"),
        P(None, "row"),
        P("row", None),
    )
    return jax.shard_map(
        functools.partial(local, mesh.shape["row"]),
        mesh=mesh,
        in_specs=placed,
        out_specs=(
            P("groups", "row"),
            P("groups", "row"),
            P("groups", "row"),
            P("groups", "row"),
            P(("groups", "row"), None),
        ),
        check_vma=False,
    )
```

```python
import functools

import jax
import jax.numpy as jnp
from jax import lax
from jax.experimental import pallas as pl
from jax.experimental.pallas import tpu as pltpu
from jax.sharding import PartitionSpec as P

F32, BF16 = jnp.float32, jnp.bfloat16
PLANES = 4


def contract_rows(left, right):
    return lax.dot_general(
        left, right, (((0,), (0,)), ((), ())), preferred_element_type=F32
    )


def contract_cols(left, right):
    return lax.dot_general(
        left, right, (((1,), (1,)), ((), ())), preferred_element_type=F32
    )


def kernel(
    x_in, dy_in, wg_hbm, wu_hbm, wd_hbm,
    out_ref, grad_ref, x_hbm, dy_hbm, h_hbm, dg_hbm, du_hbm,
    xg, dyg, wg, wu, wd, gate, up, dh, h, dg, du, ht, dgt, dut,
    keep, send_c, recv_c, send_y, recv_y, send_z, recv_z,
    wsem, az_s, az_r, ay_s, ay_r, ac_s, ac_r,
    rc_s, rc_r, ry_s, ry_r, rz_s, rz_r, osem,
):
    T, B = x_in.shape
    g = lax.axis_index("groups")
    me = lax.axis_index("row")
    c = lax.rem(me, 2)
    y = lax.rem(me // 2, 2)
    z = me // 4
    z0, z1 = lax.rem(z, 2), z // 2

    def plane(s):
        return lax.rem(z0 + s % 2, 2) + 2 * lax.rem(z1 + s // 2, 2)

    def index(zz, yy, cc):
        return (zz * 2 + yy) * 2 + cc

    def cols(block):
        return pl.ds(pl.multiple_of(block * B, B), B)

    def plane_ds(s):
        return pl.ds(pl.multiple_of(plane(s) * (4 * B), 4 * B), 4 * B)

    core_peer = (g, index(z, y, 1 - c))
    y_peer = (g, index(z, 1 - y, c))
    z_peer = [None] + [(g, index(plane(s), y, c)) for s in range(1, PLANES)]

    def weight_copy(w, s):
        sl = plane_ds(s)
        src, dst = ((wg_hbm, wg), (wu_hbm, wu), (wd_hbm, wd))[w]
        return pltpu.make_async_copy(src.at[:, sl], dst.at[:, sl], wsem.at[w, s])

    for s in range(PLANES):
        weight_copy(0, s).start()
        weight_copy(1, s).start()
    for s in range(PLANES):
        weight_copy(2, s).start()

    barrier = pltpu.get_barrier_semaphore()
    for peer in [core_peer, y_peer] + z_peer[1:]:
        pl.semaphore_signal(barrier, inc=1, device_id=peer, device_id_type=pl.DeviceIdType.MESH)
    pl.semaphore_wait(barrier, 5)

    def remote(src, dst, ss, rs, peer):
        return pltpu.make_async_remote_copy(
            src_ref=src, dst_ref=dst, send_sem=ss, recv_sem=rs,
            device_id=peer, device_id_type=pl.DeviceIdType.MESH,
        )

    ins, gathered = (x_in, dy_in), (xg, dyg)

    def hop(a, d, k):
        buf = gathered[a]
        far = z - (k - 1) if d == 0 else z + (k - 1)
        peer = (g, index(z + 1 if d == 0 else z - 1, y, c))
        sl = cols(index(far, y, c))
        src = ins[a] if k == 1 else buf.at[:, sl]
        return remote(src, buf.at[:, sl], az_s.at[a, d, k - 1], az_r.at[a, d, k - 1], peer)

    def hop_sent(d, k):
        if d == 0:
            return (z < PLANES - 1) & (z >= k - 1)
        return (z > 0) & (z + k - 1 < PLANES)

    def hop_came(d, k):
        return z >= k if d == 0 else z + k < PLANES

    def gather_copy(a, kind, zz, j=0, own=False):
        buf = gathered[a]
        sl = cols(index(zz, y if j == 0 else 1 - y, c))
        src = ins[a] if own else buf.at[:, sl]
        if kind == "y":
            return remote(src, buf.at[:, sl], ay_s.at[a, zz], ay_r.at[a, zz], y_peer)
        n = 2 * zz + j
        return remote(src, buf.at[:, sl], ac_s.at[a, n], ac_r.at[a, n], core_peer)

    def gather_begin(a):
        for d in range(2):
            @pl.when(hop_sent(d, 1))
            def _(d=d):
                hop(a, d, 1).start()
        gather_copy(a, "y", z, own=True).start()
        gather_copy(a, "c", z, own=True).start()
        gathered[a][:, cols(me)] = ins[a][...]

    def gather_z(a, k):
        buf = gathered[a]
        for d in range(2):
            @pl.when(hop_came(d, k))
            def _(d=d):
                zz = z - k if d == 0 else z + k
                sl = cols(index(zz, y, c))
                peer = (g, index(z - 1 if d == 0 else z + 1, y, c))
                view = buf.at[:, sl]
                remote(view, view, az_s.at[a, d, k - 1], az_r.at[a, d, k - 1], peer).wait_recv()
                if k < PLANES - 1:
                    @pl.when(hop_sent(d, k + 1))
                    def _():
                        hop(a, d, k + 1).start()
                gather_copy(a, "y", zz).start()
                gather_copy(a, "c", zz, 0).start()

    def gather_y(a, k):
        buf = gathered[a]

        def pass_on(zz):
            view = buf.at[:, cols(index(zz, 1 - y, c))]
            remote(view, view, ay_s.at[a, zz], ay_r.at[a, zz], y_peer).wait_recv()
            gather_copy(a, "c", zz, 1).start()

        if k == 0:
            pass_on(z)
            return
        for d in range(2):
            @pl.when(hop_came(d, k))
            def _(d=d):
                pass_on(z - k if d == 0 else z + k)

    def gather_ready(a, s):
        buf, zz = gathered[a], plane(s)
        for j, lane in ((0, y), (1, 1 - y)):
            view = buf.at[:, cols(index(zz, lane, 1 - c))]
            n = 2 * zz + j
            remote(view, view, ac_s.at[a, n], ac_r.at[a, n], core_peer).wait_recv()

    def forward(s):
        weight_copy(0, s).wait()
        weight_copy(1, s).wait()
        gather_ready(0, s)
        sl = plane_ds(s)
        x = xg[:, sl]
        gate_now = contract_cols(x, wg[:, sl])
        up_now = contract_cols(x, wu[:, sl])
        if s == 0:
            gate[...] = gate_now
            up[...] = up_now
        else:
            gate[...] += gate_now
            up[...] += up_now

    def backward(s):
        gather_ready(1, s)
        sl = plane_ds(s)
        now = contract_cols(dyg[:, sl], wd[:, sl])
        if s == 0:
            dh[...] = now
        else:
            dh[...] += now

    def reduce_c(a, s):
        return remote(send_c.at[a, s], recv_c.at[a, s], rc_s.at[a, s], rc_r.at[a, s], core_peer)

    def reduce_y(a, s):
        return remote(send_y.at[a, s], recv_y.at[a, s], ry_s.at[a, s], ry_r.at[a, s], y_peer)

    def reduce_z(a, s):
        return remote(send_z.at[a, s], recv_z.at[a, s], rz_s.at[a, s], rz_r.at[a, s], z_peer[s])

    def terms(a, block):
        sl = cols(block)
        if a == 0:
            return jnp.dot(h[...], wd[:, sl], preferred_element_type=F32)
        return jnp.dot(dg[...], wg[:, sl], preferred_element_type=F32) + jnp.dot(
            du[...], wu[:, sl], preferred_element_type=F32
        )

    def stage_c(a, s):
        for j, lane in ((1, 1 - y), (0, y)):
            send_c[a, s, j] = terms(a, index(plane(s), lane, 1 - c)).astype(BF16)
        reduce_c(a, s).start()
        for j, lane in ((1, 1 - y), (0, y)):
            keep[a, s, j] = terms(a, index(plane(s), lane, c))

    def stage_y(a, s):
        reduce_c(a, s).wait_recv()
        send_y[a, s] = (keep[a, s, 1] + recv_c[a, s, 1].astype(F32)).astype(BF16)
        reduce_y(a, s).start()
        keep[a, s, 0] += recv_c[a, s, 0].astype(F32)

    def stage_z(a, s):
        reduce_y(a, s).wait_recv()
        now = keep[a, s, 0] + recv_y[a, s].astype(F32)
        if s == 0:
            keep[a, s, 0] = now
        else:
            send_z[a, s] = now.astype(BF16)
            reduce_z(a, s).start()

    def finish(a, ref):
        total = keep[a, 0, 0]
        for s in range(1, PLANES):
            reduce_z(a, s).wait_recv()
            total += recv_z[a, s].astype(F32)
        ref[...] = total.astype(BF16)

    gather_begin(0)
    gather_z(0, 1)
    gather_y(0, 0)
    gather_z(0, 2)
    gather_begin(1)
    gather_z(0, 3)
    gather_y(0, 1)
    forward(0)
    gather_z(1, 1)
    gather_y(0, 2)
    forward(1)
    gather_y(0, 3)
    gather_z(1, 2)
    forward(2)
    gather_z(1, 3)
    gather_y(1, 0)
    forward(3)
    gather_y(1, 1)

    chunk = 32

    @pl.loop(0, T // chunk)
    def _(i):
        rows = pl.ds(pl.multiple_of(i * chunk, chunk), chunk)
        gt, u = gate[rows, :], up[rows, :]
        h[rows, :] = (gt * jax.nn.sigmoid(gt) * u).astype(BF16)

    emits = [
        pltpu.make_async_copy(src, dst, osem.at[i])
        for i, (src, dst) in enumerate(
            ((xg, x_hbm), (dyg, dy_hbm), (ht, h_hbm), (dgt, dg_hbm), (dut, du_hbm))
        )
    ]
    emits[0].start()
    for s in range(PLANES):
        weight_copy(2, s).wait()
    stage_c(0, 2)
    gather_y(1, 2)
    stage_c(0, 3)
    gather_y(1, 3)
    stage_y(0, 2)
    stage_c(0, 1)
    stage_y(0, 3)
    backward(0)
    stage_c(0, 0)
    stage_y(0, 1)
    backward(1)
    stage_z(0, 2)
    stage_y(0, 0)
    backward(2)
    stage_z(0, 3)
    backward(3)
    emits[1].start()

    @pl.loop(0, T // chunk)
    def _(i):
        rows = pl.ds(pl.multiple_of(i * chunk, chunk), chunk)
        gt, u, d = gate[rows, :], up[rows, :], dh[rows, :]
        sig = jax.nn.sigmoid(gt)
        dg[rows, :] = (d * u * sig * (1.0 + gt * (1.0 - sig))).astype(BF16)
        du[rows, :] = (d * gt * sig).astype(BF16)

    stage_c(1, 2)
    stage_z(0, 1)
    stage_c(1, 3)
    stage_y(1, 2)
    stage_c(1, 1)
    stage_y(1, 3)
    stage_c(1, 0)
    stage_y(1, 1)
    stage_z(0, 0)
    stage_z(1, 2)
    stage_y(1, 0)
    ht[...] = h[...].T
    emits[2].start()
    stage_z(1, 3)
    dgt[...] = dg[...].T
    emits[3].start()
    dut[...] = du[...].T
    emits[4].start()
    finish(0, out_ref)
    stage_z(1, 1)
    stage_z(1, 0)
    finish(1, grad_ref)

    for emit in emits:
        emit.wait()
    for a in range(2):
        for d in range(2):
            for k in range(1, PLANES):
                @pl.when(hop_sent(d, k))
                def _(a=a, d=d, k=k):
                    hop(a, d, k).wait_send()
        for s in range(PLANES):
            if s:
                reduce_z(a, s).wait_send()
            gather_copy(a, "y", s).wait_send()
            for j in range(2):
                gather_copy(a, "c", s, j).wait_send()
            reduce_c(a, s).wait_send()
            reduce_y(a, s).wait_send()


def fused(tokens, cotangent, gate_weight, up_weight, down_weight):
    T, B = tokens.shape
    F, D = down_weight.shape
    vmem = pl.BlockSpec(memory_space=pltpu.VMEM)
    hbm = pl.BlockSpec(memory_space=pl.ANY)
    dma = pltpu.SemaphoreType.DMA

    def sds(*shape):
        return jax.ShapeDtypeStruct(shape, BF16)

    pair = (2, PLANES)
    return pl.pallas_call(
        kernel,
        out_shape=(sds(T, B), sds(T, B), sds(T, D), sds(T, D), sds(F, T), sds(F, T), sds(F, T)),
        in_specs=[vmem, vmem, hbm, hbm, hbm],
        out_specs=(vmem, vmem, hbm, hbm, hbm, hbm, hbm),
        scratch_shapes=[
            pltpu.VMEM((T, D), BF16),
            pltpu.VMEM((T, D), BF16),
            pltpu.VMEM((F, D), BF16),
            pltpu.VMEM((F, D), BF16),
            pltpu.VMEM((F, D), BF16),
            pltpu.VMEM((T, F), F32),
            pltpu.VMEM((T, F), F32),
            pltpu.VMEM((T, F), F32),
            pltpu.VMEM((T, F), BF16),
            pltpu.VMEM((T, F), BF16),
            pltpu.VMEM((T, F), BF16),
            pltpu.VMEM((F, T), BF16),
            pltpu.VMEM((F, T), BF16),
            pltpu.VMEM((F, T), BF16),
            pltpu.VMEM(pair + (2, T, B), F32),
            pltpu.VMEM(pair + (2, T, B), BF16),
            pltpu.VMEM(pair + (2, T, B), BF16),
            pltpu.VMEM(pair + (T, B), BF16),
            pltpu.VMEM(pair + (T, B), BF16),
            pltpu.VMEM(pair + (T, B), BF16),
            pltpu.VMEM(pair + (T, B), BF16),
            dma((3, PLANES)),
            dma((2, 2, PLANES - 1)), dma((2, 2, PLANES - 1)), dma(pair), dma(pair),
            dma((2, 2 * PLANES)), dma((2, 2 * PLANES)),
            dma(pair), dma(pair), dma(pair), dma(pair), dma(pair), dma(pair),
            dma((5,)),
        ],
        compiler_params=pltpu.CompilerParams(
            collective_id=0, has_side_effects=True, vmem_limit_bytes=60 * 2**20
        ),
        cost_estimate=pl.CostEstimate(
            flops=12 * T * D * F, bytes_accessed=6 * D * F + 10 * T * D, transcendentals=2 * T * F
        ),
        name="swiglu_fused",
    )(tokens, cotangent, gate_weight.T, up_weight.T, down_weight)


CHUNKS = 4


def gradient_kernel(
    x_hbm, dy_hbm, ht_hbm, dgt_hbm, dut_hbm, gate_hbm, up_hbm, down_hbm,
    x, dy, ht, dgt, dut, gate_out, up_out, down_out, left_sem, right_sem, out_sem,
):
    width = x.shape[1] // CHUNKS
    lefts = [
        pltpu.make_async_copy(src, dst, left_sem.at[i])
        for i, (src, dst) in enumerate(((dgt_hbm, dgt), (dut_hbm, dut), (ht_hbm, ht)))
    ]

    def right(i, n):
        src, dst = ((x_hbm, x), (dy_hbm, dy))[i]
        sl = pl.ds(n * width, width)
        return pltpu.make_async_copy(src.at[:, sl], dst.at[:, sl], right_sem.at[i, n])

    def result(i, n):
        src, dst = ((gate_out, gate_hbm), (up_out, up_hbm), (down_out, down_hbm))[i]
        sl = pl.ds(n * width, width)
        return pltpu.make_async_copy(src.at[:, sl], dst.at[:, sl], out_sem.at[i, n])

    lefts[0].start()
    right(0, 0).start()
    lefts[1].start()
    for n in range(1, CHUNKS):
        right(0, n).start()
    lefts[2].start()
    for n in range(CHUNKS):
        right(1, n).start()

    def multiply(i, n, lhs, rhs, out):
        sl = pl.ds(n * width, width)
        out[:, sl] = jnp.dot(lhs[...], rhs[:, sl], preferred_element_type=F32).astype(BF16)
        result(i, n).start()

    for n in range(CHUNKS):
        if n == 0:
            lefts[0].wait()
        right(0, n).wait()
        multiply(0, n, dgt, x, gate_out)
        if n == 0:
            lefts[1].wait()
        multiply(1, n, dut, x, up_out)
    lefts[2].wait()
    for n in range(CHUNKS):
        right(1, n).wait()
        multiply(2, n, ht, dy, down_out)
    for i in range(3):
        for n in range(CHUNKS):
            result(i, n).wait()


def gradients(x, dy, ht, dgt, dut):
    T, D = x.shape
    F = ht.shape[0]
    hbm = pl.BlockSpec(memory_space=pl.ANY)
    dma = pltpu.SemaphoreType.DMA
    out = jax.ShapeDtypeStruct((F, D), BF16)
    return pl.pallas_call(
        gradient_kernel,
        out_shape=(out, out, out),
        in_specs=[hbm] * 5,
        out_specs=(hbm, hbm, hbm),
        scratch_shapes=[pltpu.VMEM((T, D), BF16)] * 2
        + [pltpu.VMEM((F, T), BF16)] * 3
        + [pltpu.VMEM((F, D), BF16)] * 3
        + [dma((3,)), dma((2, CHUNKS)), dma((3, CHUNKS))],
        compiler_params=pltpu.CompilerParams(vmem_limit_bytes=60 * 2**20),
        cost_estimate=pl.CostEstimate(
            flops=6 * T * D * F, bytes_accessed=6 * D * F + 4 * T * D, transcendentals=0
        ),
        name="weight_gradients",
    )(x, dy, ht, dgt, dut)


def on_device_fused(tokens, cotangent, gate_weight, up_weight, down_weight):
    output, input_grad, whole_x, whole_dy, hidden_t, d_gate_t, d_up_t = fused(
        tokens, cotangent, gate_weight, up_weight, down_weight
    )
    gate_grad, up_grad, down_grad = gradients(
        whole_x, whole_dy, hidden_t, d_gate_t, d_up_t
    )
    return (output, input_grad, gate_grad.T, up_grad.T, down_grad)


def on_device(tokens, cotangent, gate_weight, up_weight, down_weight):
    whole_x = lax.all_gather(tokens, "row", axis=1, tiled=True)
    gate = jnp.dot(whole_x, gate_weight, preferred_element_type=F32)
    up = jnp.dot(whole_x, up_weight, preferred_element_type=F32)
    sig = jax.nn.sigmoid(gate)
    hidden = (gate * sig * up).astype(BF16)
    out_terms = jnp.dot(hidden, down_weight, preferred_element_type=F32)
    output = lax.psum_scatter(out_terms, "row", scatter_dimension=1, tiled=True).astype(BF16)
    whole_dy = lax.all_gather(cotangent, "row", axis=1, tiled=True)
    d_hidden = contract_cols(whole_dy, down_weight)
    d_gate = (d_hidden * up * sig * (1.0 + gate * (1.0 - sig))).astype(BF16)
    d_up = (d_hidden * gate * sig).astype(BF16)
    gate_grad = contract_rows(whole_x, d_gate).astype(BF16)
    up_grad = contract_rows(whole_x, d_up).astype(BF16)
    down_grad = contract_rows(hidden, whole_dy).astype(BF16)
    grad_terms = contract_cols(d_gate, gate_weight) + contract_cols(d_up, up_weight)
    input_grad = lax.psum_scatter(grad_terms, "row", scatter_dimension=1, tiled=True).astype(BF16)
    return (output, input_grad, gate_grad, up_grad, down_grad)


def local(rows, tokens, cotangent, gate_weight, up_weight, down_weight):
    fits = rows == 4 * PLANES and tokens.shape[1] % 128 == 0 and tokens.shape[0] % 32 == 0
    body = on_device_fused if fits else on_device
    return body(tokens, cotangent, gate_weight, up_weight, down_weight)


def solution(mesh):
    placed = (
        P("groups", "row"),
        P("groups", "row"),
        P(None, "row"),
        P(None, "row"),
        P("row", None),
    )
    return jax.shard_map(
        functools.partial(local, mesh.shape["row"]),
        mesh=mesh,
        in_specs=placed,
        out_specs=(
            P("groups", "row"),
            P("groups", "row"),
            P("groups", "row"),
            P("groups", "row"),
            P(("groups", "row"), None),
        ),
        check_vma=False,
    )
```

```python
import functools

import jax
import jax.numpy as jnp
from jax import lax
from jax.experimental import pallas as pl
from jax.experimental.pallas import tpu as pltpu
from jax.sharding import PartitionSpec as P

F32, BF16 = jnp.float32, jnp.bfloat16
PLANES = 4


def contract_rows(left, right):
    return lax.dot_general(
        left, right, (((0,), (0,)), ((), ())), preferred_element_type=F32
    )


def contract_cols(left, right):
    return lax.dot_general(
        left, right, (((1,), (1,)), ((), ())), preferred_element_type=F32
    )


def kernel(
    x_in, dy_in, wg_hbm, wu_hbm, wd_hbm,
    out_ref, grad_ref, x_hbm, dy_hbm, h_hbm, dg_hbm, du_hbm,
    xg, dyg, wg, wu, wd, gate, up, dh, h, dg, du, ht, dgt, dut,
    keep, send_c, recv_c, send_y, recv_y, send_z, recv_z,
    wsem, az_s, az_r, ay_s, ay_r, ac_s, ac_r,
    rc_s, rc_r, ry_s, ry_r, rz_s, rz_r, osem,
):
    T, B = x_in.shape
    g = lax.axis_index("groups")
    me = lax.axis_index("row")
    c = lax.rem(me, 2)
    y = lax.rem(me // 2, 2)
    z = me // 4
    z0, z1 = lax.rem(z, 2), z // 2

    def plane(s):
        return lax.rem(z0 + s % 2, 2) + 2 * lax.rem(z1 + s // 2, 2)

    def index(zz, yy, cc):
        return (zz * 2 + yy) * 2 + cc

    def cols(block):
        return pl.ds(pl.multiple_of(block * B, B), B)

    def plane_ds(s):
        return pl.ds(pl.multiple_of(plane(s) * (4 * B), 4 * B), 4 * B)

    core_peer = (g, index(z, y, 1 - c))
    y_peer = (g, index(z, 1 - y, c))
    z_peer = [None] + [(g, index(plane(s), y, c)) for s in range(1, PLANES)]

    def weight_copy(w, s):
        sl = plane_ds(s)
        src, dst = ((wg_hbm, wg), (wu_hbm, wu), (wd_hbm, wd))[w]
        return pltpu.make_async_copy(src.at[:, sl], dst.at[:, sl], wsem.at[w, s])

    for s in range(PLANES):
        weight_copy(0, s).start()
        weight_copy(1, s).start()
    for s in range(PLANES):
        weight_copy(2, s).start()

    barrier = pltpu.get_barrier_semaphore()
    for peer in [core_peer, y_peer] + z_peer[1:]:
        pl.semaphore_signal(barrier, inc=1, device_id=peer, device_id_type=pl.DeviceIdType.MESH)
    pl.semaphore_wait(barrier, 5)

    def remote(src, dst, ss, rs, peer):
        return pltpu.make_async_remote_copy(
            src_ref=src, dst_ref=dst, send_sem=ss, recv_sem=rs,
            device_id=peer, device_id_type=pl.DeviceIdType.MESH,
        )

    ins, gathered = (x_in, dy_in), (xg, dyg)

    def hop(a, d, k):
        buf = gathered[a]
        far = z - (k - 1) if d == 0 else z + (k - 1)
        peer = (g, index(z + 1 if d == 0 else z - 1, y, c))
        sl = cols(index(far, y, c))
        src = ins[a] if k == 1 else buf.at[:, sl]
        return remote(src, buf.at[:, sl], az_s.at[a, d, k - 1], az_r.at[a, d, k - 1], peer)

    def hop_sent(d, k):
        if d == 0:
            return (z < PLANES - 1) & (z >= k - 1)
        return (z > 0) & (z + k - 1 < PLANES)

    def hop_came(d, k):
        return z >= k if d == 0 else z + k < PLANES

    def gather_copy(a, kind, zz, j=0, own=False):
        buf = gathered[a]
        sl = cols(index(zz, y if j == 0 else 1 - y, c))
        src = ins[a] if own else buf.at[:, sl]
        if kind == "y":
            return remote(src, buf.at[:, sl], ay_s.at[a, zz], ay_r.at[a, zz], y_peer)
        n = 2 * zz + j
        return remote(src, buf.at[:, sl], ac_s.at[a, n], ac_r.at[a, n], core_peer)

    def gather_begin(a):
        for d in range(2):
            @pl.when(hop_sent(d, 1))
            def _(d=d):
                hop(a, d, 1).start()
        gather_copy(a, "y", z, own=True).start()
        gather_copy(a, "c", z, own=True).start()
        gathered[a][:, cols(me)] = ins[a][...]

    def gather_z(a, k):
        buf = gathered[a]
        for d in range(2):
            @pl.when(hop_came(d, k))
            def _(d=d):
                zz = z - k if d == 0 else z + k
                sl = cols(index(zz, y, c))
                peer = (g, index(z - 1 if d == 0 else z + 1, y, c))
                view = buf.at[:, sl]
                remote(view, view, az_s.at[a, d, k - 1], az_r.at[a, d, k - 1], peer).wait_recv()
                if k < PLANES - 1:
                    @pl.when(hop_sent(d, k + 1))
                    def _():
                        hop(a, d, k + 1).start()
                gather_copy(a, "y", zz).start()
                gather_copy(a, "c", zz, 0).start()

    def gather_y(a, k):
        buf = gathered[a]

        def pass_on(zz):
            view = buf.at[:, cols(index(zz, 1 - y, c))]
            remote(view, view, ay_s.at[a, zz], ay_r.at[a, zz], y_peer).wait_recv()
            gather_copy(a, "c", zz, 1).start()

        if k == 0:
            pass_on(z)
            return
        for d in range(2):
            @pl.when(hop_came(d, k))
            def _(d=d):
                pass_on(z - k if d == 0 else z + k)

    def gather_ready(a, s):
        buf, zz = gathered[a], plane(s)
        for j, lane in ((0, y), (1, 1 - y)):
            view = buf.at[:, cols(index(zz, lane, 1 - c))]
            n = 2 * zz + j
            remote(view, view, ac_s.at[a, n], ac_r.at[a, n], core_peer).wait_recv()

    def forward(s):
        weight_copy(0, s).wait()
        weight_copy(1, s).wait()
        gather_ready(0, s)
        sl = plane_ds(s)
        x = xg[:, sl]
        gate_now = contract_cols(x, wg[:, sl])
        up_now = contract_cols(x, wu[:, sl])
        if s == 0:
            gate[...] = gate_now
            up[...] = up_now
        else:
            gate[...] += gate_now
            up[...] += up_now

    def backward(s):
        gather_ready(1, s)
        sl = plane_ds(s)
        now = contract_cols(dyg[:, sl], wd[:, sl])
        if s == 0:
            dh[...] = now
        else:
            dh[...] += now

    def reduce_c(a, s):
        return remote(send_c.at[a, s], recv_c.at[a, s], rc_s.at[a, s], rc_r.at[a, s], core_peer)

    def reduce_y(a, s):
        return remote(send_y.at[a, s], recv_y.at[a, s], ry_s.at[a, s], ry_r.at[a, s], y_peer)

    def reduce_z(a, s):
        return remote(send_z.at[a, s], recv_z.at[a, s], rz_s.at[a, s], rz_r.at[a, s], z_peer[s])

    def terms(a, block):
        sl = cols(block)
        if a == 0:
            return jnp.dot(h[...], wd[:, sl], preferred_element_type=F32)
        return jnp.dot(dg[...], wg[:, sl], preferred_element_type=F32) + jnp.dot(
            du[...], wu[:, sl], preferred_element_type=F32
        )

    def stage_c(a, s):
        for j, lane in ((1, 1 - y), (0, y)):
            send_c[a, s, j] = terms(a, index(plane(s), lane, 1 - c)).astype(BF16)
        reduce_c(a, s).start()
        for j, lane in ((1, 1 - y), (0, y)):
            keep[a, s, j] = terms(a, index(plane(s), lane, c))

    def stage_y(a, s):
        reduce_c(a, s).wait_recv()
        send_y[a, s] = (keep[a, s, 1] + recv_c[a, s, 1].astype(F32)).astype(BF16)
        reduce_y(a, s).start()
        keep[a, s, 0] += recv_c[a, s, 0].astype(F32)

    def stage_z(a, s):
        reduce_y(a, s).wait_recv()
        now = keep[a, s, 0] + recv_y[a, s].astype(F32)
        if s == 0:
            keep[a, s, 0] = now
        else:
            send_z[a, s] = now.astype(BF16)
            reduce_z(a, s).start()

    def finish(a, ref):
        total = keep[a, 0, 0]
        for s in range(1, PLANES):
            reduce_z(a, s).wait_recv()
            total += recv_z[a, s].astype(F32)
        ref[...] = total.astype(BF16)

    gather_begin(0)
    gather_z(0, 1)
    gather_y(0, 0)
    gather_z(0, 2)
    gather_begin(1)
    gather_z(0, 3)
    gather_y(0, 1)
    forward(0)
    gather_z(1, 1)
    gather_y(0, 2)
    forward(1)
    gather_y(0, 3)
    gather_z(1, 2)
    forward(2)
    gather_z(1, 3)
    gather_y(1, 0)
    forward(3)
    gather_y(1, 1)

    chunk = 32

    @pl.loop(0, T // chunk)
    def _(i):
        rows = pl.ds(pl.multiple_of(i * chunk, chunk), chunk)
        gt, u = gate[rows, :], up[rows, :]
        h[rows, :] = (gt * jax.nn.sigmoid(gt) * u).astype(BF16)

    emits = [
        pltpu.make_async_copy(src, dst, osem.at[i])
        for i, (src, dst) in enumerate(
            ((xg, x_hbm), (dyg, dy_hbm), (ht, h_hbm), (dgt, dg_hbm), (dut, du_hbm))
        )
    ]
    emits[0].start()
    for s in range(PLANES):
        weight_copy(2, s).wait()
    stage_c(0, 2)
    gather_y(1, 2)
    stage_c(0, 3)
    gather_y(1, 3)
    stage_y(0, 2)
    stage_c(0, 1)
    stage_y(0, 3)
    backward(0)
    stage_c(0, 0)
    stage_y(0, 1)
    backward(1)
    stage_z(0, 2)
    stage_y(0, 0)
    backward(2)
    stage_z(0, 3)
    backward(3)
    emits[1].start()

    @pl.loop(0, T // chunk)
    def _(i):
        rows = pl.ds(pl.multiple_of(i * chunk, chunk), chunk)
        gt, u, d = gate[rows, :], up[rows, :], dh[rows, :]
        sig = jax.nn.sigmoid(gt)
        dg[rows, :] = (d * u * sig * (1.0 + gt * (1.0 - sig))).astype(BF16)
        du[rows, :] = (d * gt * sig).astype(BF16)

    stage_c(1, 2)
    stage_z(0, 1)
    stage_c(1, 3)
    stage_y(1, 2)
    stage_c(1, 1)
    stage_y(1, 3)
    stage_c(1, 0)
    stage_y(1, 1)
    stage_z(0, 0)
    stage_z(1, 2)
    stage_y(1, 0)
    ht[...] = h[...].T
    emits[2].start()
    stage_z(1, 3)
    dgt[...] = dg[...].T
    emits[3].start()
    dut[...] = du[...].T
    emits[4].start()
    finish(0, out_ref)
    stage_z(1, 1)
    stage_z(1, 0)
    finish(1, grad_ref)

    for emit in emits:
        emit.wait()
    for a in range(2):
        for d in range(2):
            for k in range(1, PLANES):
                @pl.when(hop_sent(d, k))
                def _(a=a, d=d, k=k):
                    hop(a, d, k).wait_send()
        for s in range(PLANES):
            if s:
                reduce_z(a, s).wait_send()
            gather_copy(a, "y", s).wait_send()
            for j in range(2):
                gather_copy(a, "c", s, j).wait_send()
            reduce_c(a, s).wait_send()
            reduce_y(a, s).wait_send()


def fused(tokens, cotangent, gate_weight, up_weight, down_weight):
    T, B = tokens.shape
    F, D = down_weight.shape
    vmem = pl.BlockSpec(memory_space=pltpu.VMEM)
    hbm = pl.BlockSpec(memory_space=pl.ANY)
    dma = pltpu.SemaphoreType.DMA

    def sds(*shape):
        return jax.ShapeDtypeStruct(shape, BF16)

    pair = (2, PLANES)
    return pl.pallas_call(
        kernel,
        out_shape=(sds(T, B), sds(T, B), sds(T, D), sds(T, D), sds(F, T), sds(F, T), sds(F, T)),
        in_specs=[vmem, vmem, hbm, hbm, hbm],
        out_specs=(vmem, vmem, hbm, hbm, hbm, hbm, hbm),
        scratch_shapes=[
            pltpu.VMEM((T, D), BF16),
            pltpu.VMEM((T, D), BF16),
            pltpu.VMEM((F, D), BF16),
            pltpu.VMEM((F, D), BF16),
            pltpu.VMEM((F, D), BF16),
            pltpu.VMEM((T, F), F32),
            pltpu.VMEM((T, F), F32),
            pltpu.VMEM((T, F), F32),
            pltpu.VMEM((T, F), BF16),
            pltpu.VMEM((T, F), BF16),
            pltpu.VMEM((T, F), BF16),
            pltpu.VMEM((F, T), BF16),
            pltpu.VMEM((F, T), BF16),
            pltpu.VMEM((F, T), BF16),
            pltpu.VMEM(pair + (2, T, B), F32),
            pltpu.VMEM(pair + (2, T, B), BF16),
            pltpu.VMEM(pair + (2, T, B), BF16),
            pltpu.VMEM(pair + (T, B), BF16),
            pltpu.VMEM(pair + (T, B), BF16),
            pltpu.VMEM(pair + (T, B), BF16),
            pltpu.VMEM(pair + (T, B), BF16),
            dma((3, PLANES)),
            dma((2, 2, PLANES - 1)), dma((2, 2, PLANES - 1)), dma(pair), dma(pair),
            dma((2, 2 * PLANES)), dma((2, 2 * PLANES)),
            dma(pair), dma(pair), dma(pair), dma(pair), dma(pair), dma(pair),
            dma((5,)),
        ],
        compiler_params=pltpu.CompilerParams(
            collective_id=0, has_side_effects=True, vmem_limit_bytes=60 * 2**20
        ),
        cost_estimate=pl.CostEstimate(
            flops=12 * T * D * F, bytes_accessed=6 * D * F + 10 * T * D, transcendentals=2 * T * F
        ),
        name="swiglu_fused",
    )(tokens, cotangent, gate_weight.T, up_weight.T, down_weight)


CHUNKS = 4


def gradient_kernel(
    x_hbm, dy_hbm, ht_hbm, dgt_hbm, dut_hbm, y_in, dx_in, gate_hbm, up_hbm, down_hbm, y_out, dx_out,
    x, dy, ht, dgt, dut, gate_out, up_out, down_out, left_sem, right_sem, out_sem, pass_sem,
):
    width = x.shape[1] // CHUNKS
    lefts = [
        pltpu.make_async_copy(src, dst, left_sem.at[i])
        for i, (src, dst) in enumerate(((dgt_hbm, dgt), (dut_hbm, dut), (ht_hbm, ht)))
    ]

    def right(i, n):
        src, dst = ((x_hbm, x), (dy_hbm, dy))[i]
        sl = pl.ds(n * width, width)
        return pltpu.make_async_copy(src.at[:, sl], dst.at[:, sl], right_sem.at[i, n])

    def result(i, n):
        src, dst = ((gate_out, gate_hbm), (up_out, up_hbm), (down_out, down_hbm))[i]
        sl = pl.ds(n * width, width)
        return pltpu.make_async_copy(src.at[:, sl], dst.at[:, sl], out_sem.at[i, n])

    lefts[0].start()
    right(0, 0).start()
    lefts[1].start()
    for n in range(1, CHUNKS):
        right(0, n).start()
    lefts[2].start()
    for n in range(CHUNKS):
        right(1, n).start()
    passed = [
        pltpu.make_async_copy(y_in, y_out, pass_sem.at[0]),
        pltpu.make_async_copy(dx_in, dx_out, pass_sem.at[1]),
    ]
    for copy in passed:
        copy.start()

    def multiply(i, n, lhs, rhs, out):
        sl = pl.ds(n * width, width)
        out[:, sl] = jnp.dot(lhs[...], rhs[:, sl], preferred_element_type=F32).astype(BF16)
        result(i, n).start()

    for n in range(CHUNKS):
        if n == 0:
            lefts[0].wait()
        right(0, n).wait()
        multiply(0, n, dgt, x, gate_out)
        if n == 0:
            lefts[1].wait()
        multiply(1, n, dut, x, up_out)
    lefts[2].wait()
    for n in range(CHUNKS):
        right(1, n).wait()
        multiply(2, n, ht, dy, down_out)
    for i in range(3):
        for n in range(CHUNKS):
            result(i, n).wait()
    for copy in passed:
        copy.wait()


def gradients(x, dy, ht, dgt, dut, output, input_grad):
    T, D = x.shape
    F = ht.shape[0]
    hbm = pl.BlockSpec(memory_space=pl.ANY)
    dma = pltpu.SemaphoreType.DMA
    out = jax.ShapeDtypeStruct((F, D), BF16)
    small = jax.ShapeDtypeStruct(output.shape, BF16)
    return pl.pallas_call(
        gradient_kernel,
        out_shape=(out, out, out, small, small),
        in_specs=[hbm] * 7,
        out_specs=(hbm,) * 5,
        scratch_shapes=[pltpu.VMEM((T, D), BF16)] * 2
        + [pltpu.VMEM((F, T), BF16)] * 3
        + [pltpu.VMEM((F, D), BF16)] * 3
        + [dma((3,)), dma((2, CHUNKS)), dma((3, CHUNKS)), dma((2,))],
        compiler_params=pltpu.CompilerParams(vmem_limit_bytes=60 * 2**20),
        cost_estimate=pl.CostEstimate(
            flops=6 * T * D * F, bytes_accessed=6 * D * F + 4 * T * D, transcendentals=0
        ),
        name="weight_gradients",
    )(x, dy, ht, dgt, dut, output, input_grad)


def on_device_fused(tokens, cotangent, gate_weight, up_weight, down_weight):
    output, input_grad, whole_x, whole_dy, hidden_t, d_gate_t, d_up_t = fused(
        tokens, cotangent, gate_weight, up_weight, down_weight
    )
    gate_grad, up_grad, down_grad, output, input_grad = gradients(
        whole_x, whole_dy, hidden_t, d_gate_t, d_up_t, output, input_grad
    )
    return (output, input_grad, gate_grad.T, up_grad.T, down_grad)


def on_device(tokens, cotangent, gate_weight, up_weight, down_weight):
    whole_x = lax.all_gather(tokens, "row", axis=1, tiled=True)
    gate = jnp.dot(whole_x, gate_weight, preferred_element_type=F32)
    up = jnp.dot(whole_x, up_weight, preferred_element_type=F32)
    sig = jax.nn.sigmoid(gate)
    hidden = (gate * sig * up).astype(BF16)
    out_terms = jnp.dot(hidden, down_weight, preferred_element_type=F32)
    output = lax.psum_scatter(out_terms, "row", scatter_dimension=1, tiled=True).astype(BF16)
    whole_dy = lax.all_gather(cotangent, "row", axis=1, tiled=True)
    d_hidden = contract_cols(whole_dy, down_weight)
    d_gate = (d_hidden * up * sig * (1.0 + gate * (1.0 - sig))).astype(BF16)
    d_up = (d_hidden * gate * sig).astype(BF16)
    gate_grad = contract_rows(whole_x, d_gate).astype(BF16)
    up_grad = contract_rows(whole_x, d_up).astype(BF16)
    down_grad = contract_rows(hidden, whole_dy).astype(BF16)
    grad_terms = contract_cols(d_gate, gate_weight) + contract_cols(d_up, up_weight)
    input_grad = lax.psum_scatter(grad_terms, "row", scatter_dimension=1, tiled=True).astype(BF16)
    return (output, input_grad, gate_grad, up_grad, down_grad)


def local(rows, tokens, cotangent, gate_weight, up_weight, down_weight):
    fits = rows == 4 * PLANES and tokens.shape[1] % 128 == 0 and tokens.shape[0] % 32 == 0
    body = on_device_fused if fits else on_device
    return body(tokens, cotangent, gate_weight, up_weight, down_weight)


def solution(mesh):
    placed = (
        P("groups", "row"),
        P("groups", "row"),
        P(None, "row"),
        P(None, "row"),
        P("row", None),
    )
    return jax.shard_map(
        functools.partial(local, mesh.shape["row"]),
        mesh=mesh,
        in_specs=placed,
        out_specs=(
            P("groups", "row"),
            P("groups", "row"),
            P("groups", "row"),
            P("groups", "row"),
            P(("groups", "row"), None),
        ),
        check_vma=False,
    )
```
